256 devices in a mesh: row: 8 (over z_hi, core), col: 8 (over x, z_lo), depth: 4 (over y).
Axes of the slice: x: 4, y: 4, z: 8 (z_hi: 4, z_lo: 2; z = z_hi * 2 + z_lo), core: 2. Of those that a mesh axis runs over, the one named last changes fastest.
Arguments:
- tokens: bfloat16 [4096, 6144], P(('depth', 'col'), 'row'), may hold values from -6 to 6
- up_weight: bfloat16 [6144, 24576], P('row', 'col'), may hold values from -0.078125 to 0.078125
- hidden_bias: bfloat16 [24576], P('col'), may hold values from -3 to 3
- act_grad: bfloat16 [4096, 24576], P(('depth', 'row'), 'col'), may hold values from -1.1953125 to 1.1953125
Outputs:
- activation: bfloat16 [4096, 24576], P(('depth', 'row'), 'col')
- token_grad: bfloat16 [4096, 6144], P(('depth', 'col'), 'row')
- weight_grad: float32 [6144, 24576], P('row', ('col', 'depth'))
- bias_grad: float32 [24576], P('col')
The draws below stay inside these ranges and needn't reach their ends.
All inputs are finite; a program needn't handle non-finite values.
Results may differ from the reference program's by a relative error of at most 0.0065.
Values may be sent and summed in bfloat16 or wider, within the bound.
No kernel may reach another device: no remote copies, remote signals or barrier semaphores. Data moves between devices by JAX's collectives and lax.ppermute only.
A program may use at most 128 MiB of HBM per device.

```python
import math
import jax
import jax.numpy as jnp
from jax import lax

D = 6144
FF = 24576
TOKENS = 4096


def steps_of(key, dims, split, low, top_value):
    loudness = 1.0
    for position, blocks in split:
        heights = jax.random.uniform(jax.random.fold_in(jax.random.fold_in(key, 6), position), (blocks,), jnp.float32, low / len(split), top_value / len(split))
        loudness = loudness * jnp.repeat(jnp.exp(heights), dims[position] // blocks).reshape((-1,) + (1,) * (len(dims) - 1 - position))
    return loudness


def centred(own_key, extent, deviation, most, cuts=(), dtype=jnp.bfloat16):
    level = steps_of(own_key, extent, cuts, -0.22, 0.18) if cuts else 1.0
    array = jax.random.normal(own_key, extent, jnp.float32) * deviation * level
    return jnp.minimum(jnp.maximum(array, -most), most).astype(dtype)


def setup_inputs(seed: int = 0) -> dict:
    keys = jax.random.split(jax.random.key(seed), 5)
    return {
        "tokens": centred(keys[0], (TOKENS, D), 1.0, 6.0, ((0, 32), (1, 8))),
        "up_weight": centred(keys[1], (D, FF), D ** -0.5, 0.078125, ((0, 8), (1, 8))),
        "hidden_bias": centred(keys[2], (FF,), 0.5, 3.0, ((0, 8),)),
        "act_grad": centred(keys[3], (TOKENS, FF), 0.2, 1.1953125, ((0, 32), (1, 8))),
    }


gelu_coef = math.sqrt(2.0 / math.pi)

def gelu_parts(preact):
    inner_arg = gelu_coef * (preact + 0.044715 * preact * preact * preact)
    tanh_val = jnp.tanh(inner_arg)
    activation = 0.5 * preact * (1.0 + tanh_val)
    slopes = 0.5 * (1.0 + tanh_val) + 0.5 * preact * (1.0 - tanh_val * tanh_val) * gelu_coef * (1.0 + 3.0 * 0.044715 * preact * preact)
    return (activation, slopes)

def reference(tokens, up_weight, hidden_bias, act_grad):
    preact = jnp.dot(tokens, up_weight, preferred_element_type=jnp.float32) + hidden_bias.astype(jnp.float32)[None, :]
    activation, slopes = gelu_parts(preact)
    pre_grad = (act_grad.astype(jnp.float32) * slopes).astype(jnp.bfloat16)
    token_grad = lax.dot_general(pre_grad, up_weight, (((1,), (1,)), ((), ())), preferred_element_type=jnp.float32).astype(jnp.bfloat16)
    weight_grad = lax.dot_general(tokens, pre_grad, (((0,), (0,)), ((), ())), preferred_element_type=jnp.float32)
    bias_grad = lax.optimization_barrier(jnp.sum(pre_grad.astype(jnp.float32), axis=0))
    return (activation.astype(jnp.bfloat16), token_grad, weight_grad, bias_grad)
```

```python
import math

import jax
import jax.numpy as jnp
from jax import lax
from jax.experimental import pallas as pl
from jax.experimental.pallas import tpu as pltpu
from jax.sharding import PartitionSpec as P

gelu_coef = math.sqrt(2.0 / math.pi)
f32 = jnp.float32
bf16 = jnp.bfloat16

ORDER = (1, 3, 2, 0)
WIDTH = 384
PARTS = ((0, 64), (64, 128))
ROUNDS = ((0, 0, 2), (0, 2, 4), (1, 0, 2), (1, 2, 3), (1, 3, 4))


def gelu_parts(preact):
    inner_arg = gelu_coef * (preact + 0.044715 * preact * preact * preact)
    tanh_val = jnp.tanh(inner_arg)
    activation = 0.5 * preact * (1.0 + tanh_val)
    slopes = 0.5 * (1.0 + tanh_val) + 0.5 * preact * (1.0 - tanh_val * tanh_val) * gelu_coef * (
        1.0 + 3.0 * 0.044715 * preact * preact
    )
    return (activation, slopes)


def shift_z(v, by):
    return lax.ppermute(v, "row", [(i, (i + 2 * by) % 8) for i in range(8)])


def swap_core(v):
    return lax.ppermute(v, "row", [(i, i ^ 1) for i in range(8)])


def shift_x(v, by):
    return lax.ppermute(v, "col", [(i, (i + 2 * by) % 8) for i in range(8)])


def swap_z(v):
    return lax.ppermute(v, "col", [(i, i ^ 1) for i in range(8)])


def shift_y(v, by):
    return lax.ppermute(v, "depth", [(i, (i + by) % 4) for i in range(4)])


def split_columns(source, places):
    rows, columns = source.shape
    count = places.shape[0] // 2
    width = columns // places.shape[0]

    def kernel(places_ref, first_in, second_in, first_out, second_out):
        first_out[...] = first_in[...]
        second_out[...] = second_in[...]

    out = jax.ShapeDtypeStruct((rows, count * width), source.dtype)
    return pl.pallas_call(
        kernel,
        grid_spec=pltpu.PrefetchScalarGridSpec(
            num_scalar_prefetch=1,
            grid=(count,),
            in_specs=[
                pl.BlockSpec((rows, width), lambda i, at: (0, at[i])),
                pl.BlockSpec((rows, width), lambda i, at: (0, at[i + count])),
            ],
            out_specs=[pl.BlockSpec((rows, width), lambda i, at: (0, i))] * 2,
        ),
        out_shape=[out, out],
        cost_estimate=pl.CostEstimate(flops=0, bytes_accessed=2 * source.size * source.dtype.itemsize, transcendentals=0),
    )(places, source, source)


def join_columns(first, second, places):
    rows, columns = first.shape
    count = places.shape[0] // 2
    width = columns // count

    def kernel(places_ref, first_in, second_in, out):
        @pl.when(pl.program_id(0) < count)
        def _():
            out[...] = first_in[...]

        @pl.when(pl.program_id(0) >= count)
        def _():
            out[...] = second_in[...]

    return pl.pallas_call(
        kernel,
        grid_spec=pltpu.PrefetchScalarGridSpec(
            num_scalar_prefetch=1,
            grid=(2 * count,),
            in_specs=[
                pl.BlockSpec((rows, width), lambda i, at: (0, jnp.minimum(i, count - 1))),
                pl.BlockSpec((rows, width), lambda i, at: (0, jnp.maximum(i - count, 0))),
            ],
            out_specs=pl.BlockSpec((rows, width), lambda i, at: (0, at[i])),
        ),
        out_shape=jax.ShapeDtypeStruct((rows, 2 * columns), first.dtype),
        cost_estimate=pl.CostEstimate(flops=0, bytes_accessed=4 * first.size * first.dtype.itemsize, transcendentals=0),
    )(places, first, second)


def turned(blocks, by):
    n = blocks.shape[0]
    return lax.dynamic_slice_in_dim(jnp.concatenate([blocks, blocks[: n - 1]]), by % n, n, 0)


def after(values, done):
    if done is None:
        return values
    return lax.optimization_barrier((values, done))[0]


def body(tokens, up_weight, hidden_bias, act_grad):
    at_row, at_col, y = lax.axis_index("row"), lax.axis_index("col"), lax.axis_index("depth")
    z, core, x, low = at_row // 2, at_row % 2, at_col // 2, at_col % 2
    group = (y + jnp.array(ORDER, dtype=jnp.int32)) % 4
    places = jnp.concatenate([2 * group + core, 2 * group + 1 - core]).astype(jnp.int32)

    def in_order(mine, other, at):
        return jnp.where(at == 0, jnp.concatenate([mine, other]), jnp.concatenate([other, mine]))

    def gather_pair(part):
        with jax.named_scope("tokens"):
            own = tokens[slice(*PARTS[part])]
            return in_order(own, swap_z(own), low)

    def gather_x(pair):
        with jax.named_scope("tokens"):
            return [pair, shift_x(pair, -1), shift_x(pair, 2), shift_x(pair, 1)]

    def gather_core(around):
        with jax.named_scope("tokens"):
            mine = turned(jnp.stack(around), z - x)
            both = jnp.concatenate([mine, swap_core(mine)], axis=-1)
            return both.reshape(-1, both.shape[-1])

    pair = gather_pair(0)
    with jax.named_scope("weights"):
        kept, sent = split_columns(up_weight, places)
        received = swap_core(sent)
    around = gather_x(pair)
    with jax.named_scope("weights"):
        weights = {
            cut: jnp.concatenate([part[:, cut[0] * WIDTH : cut[1] * WIDTH] for part in (kept, received)])
            for cut in ((0, 2), (2, 4), (2, 3), (3, 4))
        }
    gathered = [gather_core(around), None]

    def up(k, done):
        part, low_group, high_group = ROUNDS[k]
        with jax.named_scope("up"):
            here = after(gathered[part], done)
            return jnp.dot(here, weights[low_group, high_group], preferred_element_type=f32).astype(bf16)

    def block(partial, j):
        return partial.reshape(4, -1, partial.shape[-1])[j % 4]

    def reduce_first(partial, turn):
        with jax.named_scope("reduce"):
            return shift_z(block(partial, 2), turn), shift_z(block(partial, -turn), -turn)

    def reduce_second(partial, passed, turn, done):
        with jax.named_scope("reduce"):
            passed = after(passed, done)
            return shift_z((block(partial, turn).astype(f32) + passed.astype(f32)).astype(bf16), turn)

    def gather_first(grad, turn):
        with jax.named_scope("gather"):
            return shift_z(grad, -turn), shift_z(grad, turn)

    def gather_second(near, turn, done):
        with jax.named_scope("gather"):
            return shift_z(after(near, done), turn)

    def gather_all(grad, near, passed, far, turn):
        blocks = [grad, None, far, None]
        blocks[turn % 4] = near
        blocks[-turn % 4] = passed
        return blocks

    def middle(k, partial, far, near, done):
        part, low_group, high_group = ROUNDS[k]
        cut = slice(low_group * WIDTH, high_group * WIDTH)
        with jax.named_scope("gelu"):
            far = after(far, done)
            preact = block(partial, 0).astype(f32) + far.astype(f32) + near.astype(f32) + biases[:, cut]
            activation, slopes = gelu_parts(preact)
            grad = (act_grads[part][:, cut].astype(f32) * slopes).astype(bf16)
            activations[k] = activation.astype(bf16)
            return grad

    def back(k, grads, done):
        part, low_group, high_group = ROUNDS[k]
        with jax.named_scope("back"):
            here, _ = lax.optimization_barrier((jnp.concatenate(grads), done))
            term = lax.dot_general(
                here, weights[low_group, high_group], (((1,), (1,)), ((), ())), preferred_element_type=f32
            )
            token_sum = term if token_sums[part] is None else token_sums[part] + term
            token_sums[part] = token_sum
            here = after(here, token_sum)
            sums = jnp.sum(here.astype(f32).reshape(4, -1, here.shape[-1]), axis=1)
            sums = (sums[0] + sums[2]) + (sums[1] + sums[3])
            weight_sum = lax.dot_general(gathered[part], here, (((0,), (0,)), ((), ())), preferred_element_type=f32)
            return token_sum, weight_sum, sums

    def token_core(part):
        with jax.named_scope("token_grad"):
            half = token_sums[part].shape[1] // 2
            return swap_core(token_sums[part][:, half:].astype(bf16))

    def token_x(part, other, done):
        with jax.named_scope("token_grad"):
            half = token_sums[part].shape[1] // 2
            other = after(other, done)
            total = (token_sums[part][:, :half] + other.astype(f32)).astype(bf16)
            total = turned(total.reshape(4, -1, half), x - z)
            return [total[0]] + [shift_x(total[i], i) for i in (1, 2, 3)]

    def token_z(terms, done):
        with jax.named_scope("token_grad"):
            terms = after(terms, done)
            total = sum(t.astype(f32) for t in terms)
            rows = total.shape[0] // 2
            keep = jnp.where(low == 0, total[:rows], total[rows:])
            give = jnp.where(low == 0, total[rows:], total[:rows])
            return keep, swap_z(give.astype(bf16))

    def token_last(keep, other):
        with jax.named_scope("token_grad"):
            return (keep + other.astype(f32)).astype(bf16)

    activations = {}
    token_sums = [None, None]
    reduce_turn = (1, -1, -1, -1, -1)
    gather_turn = (1, 1, 1, 1, -1)

    first = up(0, None)
    r0 = reduce_first(first, reduce_turn[0])
    second = up(1, first)
    r1 = reduce_first(second, reduce_turn[1])
    pair = gather_pair(1)
    around = gather_x(after(pair, second))
    with jax.named_scope("split"):
        kept, sent = split_columns(after(act_grad, second), places)
        other = swap_core(sent)
        upper, lower = jnp.where(core == 0, kept, other), jnp.where(core == 0, other, kept)
        act_grads = [jnp.concatenate([upper[slice(*p)], lower[slice(*p)]]) for p in PARTS]
        biases, _ = split_columns(after(hidden_bias, second).astype(f32)[None, :], places)
    far0 = reduce_second(first, r0[0], reduce_turn[0], second)
    gathered[1] = gather_core(around)
    far1 = reduce_second(second, r1[0], reduce_turn[1], far0)
    grad0 = middle(0, first, far0, r0[1], r1[0])
    g0 = gather_first(grad0, gather_turn[0])
    third = up(2, grad0)
    r2 = reduce_first(third, reduce_turn[2])
    far_g0 = gather_second(g0[1], gather_turn[0], third)
    far2 = reduce_second(third, r2[0], reduce_turn[2], g0[1])
    grad1 = middle(1, second, far1, r1[1], r2[0])
    g1 = gather_first(grad1, gather_turn[1])
    fourth = up(3, grad1)
    r3 = reduce_first(fourth, reduce_turn[3])
    tsum, wsum0, sums0 = back(0, gather_all(grad0, *g0, far_g0, gather_turn[0]), fourth)
    far_g1 = gather_second(g1[1], gather_turn[1], wsum0)
    far3 = reduce_second(fourth, r3[0], reduce_turn[3], g1[1])
    grad2 = middle(2, third, far2, r2[1], r3[0])
    g2 = gather_first(grad2, gather_turn[2])
    fifth = up(4, grad2)
    r4 = reduce_first(fifth, reduce_turn[4])
    tsum, wsum1, sums1 = back(1, gather_all(grad1, *g1, far_g1, gather_turn[1]), fifth)
    other_a = token_core(0)
    far_g2 = gather_second(g2[1], gather_turn[2], wsum1)
    far4 = reduce_second(fifth, r4[0], reduce_turn[4], g2[1])
    grad3 = middle(3, fourth, far3, r3[1], r4[0])
    g3 = gather_first(grad3, gather_turn[3])
    terms_a = token_x(0, other_a, grad3)
    tsum, wsum2, sums2 = back(2, gather_all(grad2, *g2, far_g2, gather_turn[2]), terms_a[0])
    with jax.named_scope("weight_grad"):
        total = wsum0 + wsum2
        y1 = shift_y(total[:, :WIDTH].astype(bf16), 1)
        y3 = shift_y(total[:, WIDTH:].astype(bf16), 3)
    far_g3 = gather_second(g3[1], gather_turn[3], wsum2)
    grad4 = middle(4, fifth, far4, r4[1], g3[1])
    g4 = gather_first(grad4, gather_turn[4])
    keep_a, zother_a = token_z(terms_a, grad4)
    tsum, wsum3, sums3 = back(3, gather_all(grad3, *g3, far_g3, gather_turn[3]), keep_a)
    with jax.named_scope("weight_grad"):
        y2 = shift_y((wsum1[:, :WIDTH] + wsum3).astype(bf16), 2)
    far_g4 = gather_second(g4[1], gather_turn[4], wsum3)
    with jax.named_scope("activation"):
        early = jnp.concatenate([activations[0], activations[1]], axis=1)
        late = jnp.concatenate([activations[2], activations[3], activations[4]], axis=1)
        early, late = after((early, late), g4[1])
        rows = early.shape[0] // 2
        keep = jnp.where(core == 0, jnp.concatenate([early[:rows], late[:rows]]), jnp.concatenate([early[rows:], late[rows:]]))
        give = jnp.where(core == 0, jnp.concatenate([early[rows:], late[rows:]]), jnp.concatenate([early[:rows], late[:rows]]))
        activation = join_columns(keep, swap_core(give), places)
    tsum, wsum4, sums4 = back(4, gather_all(grad4, *g4, far_g4, gather_turn[4]), wsum3)
    other_b = token_core(1)
    with jax.named_scope("weight_grad"):
        total = wsum1[:, WIDTH:] + wsum4 + y1.astype(f32) + y2.astype(f32) + y3.astype(f32)
        half = total.shape[0] // 2
        other = swap_core(total[half:])
        mine = total[:half]
        weight_grad = join_columns(mine, other, jnp.stack([core, 1 - core]).astype(jnp.int32))
    terms_b = token_x(1, other_b, None)
    keep_b, zother_b = token_z(terms_b, None)
    token_grad = jnp.concatenate([token_last(keep_a, zother_a), token_last(keep_b, zother_b)])
    with jax.named_scope("bias_grad"):
        mine = jnp.concatenate([sums0, sums1]) + jnp.concatenate([sums2, sums3, sums4])
        sums = join_columns(mine[None], swap_core(mine)[None], places)[0]
        opposite = sums + shift_y(sums, 2)
        bias_grad = opposite + shift_y(opposite, 1)
    return (activation, token_grad, weight_grad, bias_grad)


def solution(mesh):
    placed = (P(("depth", "col"), "row"), P("row", "col"), P("col"), P(("depth", "row"), "col"))
    return jax.shard_map(
        body,
        mesh=mesh,
        in_specs=placed,
        out_specs=(
            P(("depth", "row"), "col"),
            P(("depth", "col"), "row"),
            P("row", ("col", "depth")),
            P("col"),
        ),
        check_vma=False,
    )
```

```python
import math

import jax
import jax.numpy as jnp
from jax import lax
from jax.experimental import pallas as pl
from jax.experimental.pallas import tpu as pltpu
from jax.sharding import PartitionSpec as P

gelu_coef = math.sqrt(2.0 / math.pi)
f32 = jnp.float32
bf16 = jnp.bfloat16

ORDER = (1, 3, 2, 0)
WIDTH = 384
PARTS = ((0, 64), (64, 128))
ROUNDS = ((0, 0, 2), (1, 0, 2), (0, 2, 4), (1, 2, 4))
SUM_SIDE = (1, -1)
PIECES = ((0, 0, 2, 1), (1, 0, 2, -1), (2, 2, 4, 1), (3, 2, 4, -1))
CORES = [[0, 2, 4, 6], [1, 3, 5, 7]]


def gelu_parts(preact):
    inner_arg = gelu_coef * (preact + 0.044715 * preact * preact * preact)
    tanh_val = jnp.tanh(inner_arg)
    activation = 0.5 * preact * (1.0 + tanh_val)
    slopes = 0.5 * (1.0 + tanh_val) + 0.5 * preact * (1.0 - tanh_val * tanh_val) * gelu_coef * (
        1.0 + 3.0 * 0.044715 * preact * preact
    )
    return (activation, slopes)


def shift_z(v, by):
    return lax.ppermute(v, "row", [(i, (i + 2 * by) % 8) for i in range(8)])


def swap_core(v):
    return lax.ppermute(v, "row", [(i, i ^ 1) for i in range(8)])


def shift_x(v, by):
    return lax.ppermute(v, "col", [(i, (i + 2 * by) % 8) for i in range(8)])


def swap_z(v):
    return lax.ppermute(v, "col", [(i, i ^ 1) for i in range(8)])


def shift_y(v, by):
    return lax.ppermute(v, "depth", [(i, (i + by) % 4) for i in range(4)])


def split_columns(source, places):
    rows, columns = source.shape
    count = places.shape[0] // 2
    width = columns // places.shape[0]

    def kernel(places_ref, first_in, second_in, first_out, second_out):
        first_out[...] = first_in[...]
        second_out[...] = second_in[...]

    out = jax.ShapeDtypeStruct((rows, count * width), source.dtype)
    return pl.pallas_call(
        kernel,
        grid_spec=pltpu.PrefetchScalarGridSpec(
            num_scalar_prefetch=1,
            grid=(count,),
            in_specs=[
                pl.BlockSpec((rows, width), lambda i, at: (0, at[i])),
                pl.BlockSpec((rows, width), lambda i, at: (0, at[i + count])),
            ],
            out_specs=[pl.BlockSpec((rows, width), lambda i, at: (0, i))] * 2,
        ),
        out_shape=[out, out],
        cost_estimate=pl.CostEstimate(flops=0, bytes_accessed=2 * source.size * source.dtype.itemsize, transcendentals=0),
    )(places, source, source)


def split_small(source, places):
    rows, columns = source.shape
    count = places.shape[0] // 2
    width = columns // places.shape[0]
    tile = min(rows, 128)

    def kernel(at, source_ref, *refs):
        for half, out in enumerate(refs[-2:]):
            for i in range(count):
                start = pl.multiple_of(at[half * count + i] * width, 128)
                out[:, i * width : (i + 1) * width] = source_ref[:, pl.ds(start, width)]

    out = jax.ShapeDtypeStruct((rows, count * width), source.dtype)
    return pl.pallas_call(
        kernel,
        grid_spec=pltpu.PrefetchScalarGridSpec(
            num_scalar_prefetch=1,
            grid=(rows // tile,),
            in_specs=[pl.BlockSpec((tile, columns), lambda i, at: (i, 0))],
            out_specs=[pl.BlockSpec((tile, count * width), lambda i, at: (i, 0))] * 2,
        ),
        out_shape=[out, out],
    )(places, source)


def join_columns(first, second, places):
    rows, columns = first.shape
    count = places.shape[0] // 2
    width = columns // count
    tile = min(rows, 128)

    def kernel(at, first_ref, second_ref, *refs):
        for half, source in enumerate((first_ref, second_ref)):
            for i in range(count):
                start = pl.multiple_of(at[half * count + i] * width, 128)
                refs[-1][:, pl.ds(start, width)] = source[:, i * width : (i + 1) * width]

    return pl.pallas_call(
        kernel,
        grid_spec=pltpu.PrefetchScalarGridSpec(
            num_scalar_prefetch=1,
            grid=(rows // tile,),
            in_specs=[pl.BlockSpec((tile, columns), lambda i, at: (i, 0))] * 2,
            out_specs=pl.BlockSpec((tile, 2 * columns), lambda i, at: (i, 0)),
        ),
        out_shape=jax.ShapeDtypeStruct((rows, 2 * columns), first.dtype),
    )(places, first, second)


def turned(blocks, by):
    n = blocks.shape[0]
    return lax.dynamic_slice_in_dim(jnp.concatenate([blocks, blocks[: n - 1]]), by % n, n, 0)


def after(values, done):
    if done is None:
        return values
    return lax.optimization_barrier((values, done))[0]


def body(tokens, up_weight, hidden_bias, act_grad):
    at_row, at_col, y = lax.axis_index("row"), lax.axis_index("col"), lax.axis_index("depth")
    z, core, x, low = at_row // 2, at_row % 2, at_col // 2, at_col % 2
    group = (y + jnp.array(ORDER, dtype=jnp.int32)) % 4
    places = jnp.concatenate([2 * group + core, 2 * group + 1 - core]).astype(jnp.int32)

    def in_order(mine, other, at):
        return jnp.where(at == 0, jnp.concatenate([mine, other]), jnp.concatenate([other, mine]))

    def gather_pair(part):
        with jax.named_scope("tokens"):
            own = tokens[slice(*PARTS[part])]
            return in_order(own, swap_z(own), low)

    def gather_x(pair):
        with jax.named_scope("tokens"):
            return [pair, shift_x(pair, -1), shift_x(pair, 2), shift_x(pair, 1)]

    def gather_core(around):
        with jax.named_scope("tokens"):
            mine = turned(jnp.stack(around), z - x)
            both = jnp.concatenate([mine, swap_core(mine)], axis=-1)
            return both.reshape(-1, both.shape[-1])

    pair = gather_pair(0)
    with jax.named_scope("weights"):
        kept, sent = split_columns(up_weight, places)
        received = swap_core(sent)
    around = gather_x(after(pair, kept))
    with jax.named_scope("split"):
        kept_grad, sent_grad = split_small(act_grad, places)
        other_grad = swap_core(sent_grad)
        biases, _ = split_small(hidden_bias.astype(f32)[None, :], places)
        around = after(around, (kept_grad, biases))
    with jax.named_scope("weights"):
        weights = {
            cut: jnp.concatenate([part[:, cut[0] * WIDTH : cut[1] * WIDTH] for part in (kept, received)])
            for cut in ((0, 2), (2, 4))
        }
    gathered = [gather_core(around), None]
    activations, column_sums, grads = {}, {}, {}
    token_sums = [None, None]

    def up(k, done):
        part, low_group, high_group = ROUNDS[k]
        with jax.named_scope("up"):
            here = gathered[part] if done is None else after(gathered[part], done)
            return jnp.dot(here, weights[low_group, high_group], preferred_element_type=f32).astype(bf16)

    def scatter(partial):
        with jax.named_scope("sum"):
            natural = turned(partial.reshape(4, -1, partial.shape[-1]), -z).reshape(partial.shape)
            return natural, lax.psum_scatter(natural, "row", scatter_dimension=0, axis_index_groups=CORES, tiled=True)

    def block(partial, j):
        return partial.reshape(4, -1, partial.shape[-1])[j % 4]

    def sum_first(k, partial):
        with jax.named_scope("sum"):
            far, near = lax.optimization_barrier((block(partial, 2), block(partial, -SUM_SIDE[k])))
            return far, shift_z(far, SUM_SIDE[k]), shift_z(near, -SUM_SIDE[k])

    def sum_second(k, partial, passed, near, done):
        with jax.named_scope("sum"):
            passed = after(passed, (near, done))
            total = (block(partial, SUM_SIDE[k]).astype(f32) + passed.astype(f32)).astype(bf16)
            return total, shift_z(total, SUM_SIDE[k])

    def middle(i, terms, done):
        k, low_group, high_group, _ = PIECES[i]
        part, first_group, _ = ROUNDS[k]
        cut = slice(low_group * WIDTH, high_group * WIDTH)
        mine = slice((low_group - first_group) * WIDTH, (high_group - first_group) * WIDTH)
        with jax.named_scope("gelu"):
            terms = [after(terms[0], done)] + terms[1:]
            preact = sum(t[:, mine].astype(f32) for t in terms) + biases[:, cut]
            activation, slopes = gelu_parts(preact)
            grad = (act_grads[part][:, cut].astype(f32) * slopes).astype(bf16)
            grads[i], activations[i] = grad, activation.astype(bf16)
            return grad

    def gather_first(i, done=None):
        side = PIECES[i][3]
        with jax.named_scope("gather"):
            grad = grads[i] if done is None else after(grads[i], done)
            return shift_z(grad, -side), shift_z(grad, side)

    def gather_second(i, near, passed, done):
        side = PIECES[i][3]
        with jax.named_scope("gather"):
            passed, near = after((passed, near), done)
            if i < len(PIECES) - 1:
                passed = after(passed, near)
                far = shift_z(passed, side)
            else:
                half = passed.shape[1] // 2
                far = shift_z(passed[:, :half], side), shift_z(near[:, half:], -side)
                far = jnp.concatenate(far, axis=1)
            blocks = [grads[i], None, far, None]
            blocks[side % 4], blocks[-side % 4] = near, passed
            return passed, blocks

    def whole(blocks, done):
        with jax.named_scope("gather"):
            return lax.optimization_barrier((jnp.concatenate(blocks), done))[0]

    def down(i, here):
        k, low_group, high_group, _ = PIECES[i]
        part = ROUNDS[k][0]
        with jax.named_scope("down"):
            term = lax.dot_general(
                here, weights[low_group, high_group], (((1,), (1,)), ((), ())), preferred_element_type=f32
            )
            token_sums[part] = term if token_sums[part] is None else token_sums[part] + term
            return token_sums[part]

    def weigh(i, here, before=None):
        with jax.named_scope("weight_grad"):
            tokens_here = gathered[ROUNDS[PIECES[i][0]][0]]
            term = lax.dot_general(tokens_here, here, (((0,), (0,)), ((), ())), preferred_element_type=f32)
            return term if before is None else before + term

    def add_up(i, here):
        with jax.named_scope("bias_grad"):
            sums = jnp.sum(here.astype(f32).reshape(4, -1, here.shape[-1]), axis=1)
            column_sums[i] = (sums[0] + sums[2]) + (sums[1] + sums[3])
            return column_sums[i]

    def token_core(part):
        with jax.named_scope("token_grad"):
            half = token_sums[part].shape[1] // 2
            operand = token_sums[part][:, half:].astype(bf16)
            return operand, swap_core(operand)

    def token_x(part, other, done):
        with jax.named_scope("token_grad"):
            half = token_sums[part].shape[1] // 2
            other = after(other, done)
            total = (token_sums[part][:, :half] + other.astype(f32)).astype(bf16)
            total = turned(total.reshape(4, -1, half), x - z)
            return total, [total[0]] + [shift_x(total[i], i) for i in (1, 2, 3)]

    def token_z(terms, done):
        with jax.named_scope("token_grad"):
            terms = after(terms, done)
            total = sum(t.astype(f32) for t in terms)
            rows = total.shape[0] // 2
            keep = jnp.where(low == 0, total[:rows], total[rows:])
            give = jnp.where(low == 0, total[rows:], total[:rows])
            return keep, swap_z(give.astype(bf16))

    def token_last(keep, other):
        with jax.named_scope("token_grad"):
            return (keep + other.astype(f32)).astype(bf16)

    partial0 = up(0, None)
    far0, passed0, near0 = sum_first(0, partial0)
    partial2 = up(2, far0)
    natural2, preact2 = scatter(partial2)
    pair = gather_pair(1)
    around = gather_x(after(pair, far0))
    done, far0 = sum_second(0, partial0, passed0, near0, natural2)
    gathered[1] = gather_core(after(around, done))
    partial1 = up(1, None)
    far1, passed1, near1 = sum_first(1, partial1)
    partial3 = up(3, far1)
    natural3, preact3 = scatter(partial3)
    with jax.named_scope("split"):
        other_grad = after(other_grad, done)
        upper, lower = jnp.where(core == 0, kept_grad, other_grad), jnp.where(core == 0, other_grad, kept_grad)
        act_grads = [jnp.concatenate([upper[slice(*p)], lower[slice(*p)]]) for p in PARTS]
    done = middle(0, [far0, near0, block(partial0, 0)], natural3)
    first0 = gather_first(0)
    done, far1 = sum_second(1, partial1, passed1, near1, done)
    done, blocks0 = gather_second(0, *first0, done)
    done = middle(1, [far1, near1, block(partial1, 0)], done)
    first1 = gather_first(1)
    done = middle(2, [preact2], done)
    here0 = whole(blocks0, done)
    weight_sum0 = weigh(0, after(here0, down(0, here0)))
    add_up(0, here0)
    done, blocks1 = gather_second(1, *first1, weight_sum0)
    first2 = gather_first(2, done)
    here1 = whole(blocks1, done)
    weight_sum1 = weigh(1, here1, weight_sum0)
    with jax.named_scope("weight_grad"):
        sent1, sent3 = weight_sum1[:, :WIDTH].astype(bf16), weight_sum1[:, WIDTH:].astype(bf16)
        sent1, sent3 = lax.optimization_barrier((sent1, sent3))
        y1, y3 = shift_y(sent1, 1), shift_y(sent3, 3)
    done = middle(3, [preact3], (sent1, sent3))
    done, blocks2 = gather_second(2, *first2, done)
    first3 = gather_first(3, done)
    done = down(1, after(here1, done))
    add_up(1, here1)
    here2 = whole(blocks2, done)
    down(2, here2)
    done, other_a = token_core(0)
    weight_sum2 = weigh(2, after(here2, done))
    add_up(2, here2)
    with jax.named_scope("activation"):
        pieces = [jnp.concatenate([activations[i], activations[i + 2]], axis=1) for i in (0, 1)]
        rows = pieces[0].shape[0] // 2
        upper = jnp.concatenate([p[:rows] for p in pieces])
        lower = jnp.concatenate([p[rows:] for p in pieces])
        keep, give = jnp.where(core == 0, upper, lower), jnp.where(core == 0, lower, upper)
        keep, give = after((keep, give), weight_sum2)
        other = swap_core(give)
    done, blocks3 = gather_second(3, *first3, (keep, give))
    done, terms_a = token_x(0, other_a, done)
    with jax.named_scope("activation"):
        activation = join_columns(after(keep, done), other, places)
    here3 = whole(blocks3, (done, activation))
    with jax.named_scope("weight_grad"):
        sent2 = lax.optimization_barrier(weigh(3, here3[:, :WIDTH], weight_sum2[:, :WIDTH]).astype(bf16))
        y2 = shift_y(sent2, 2)
    down(3, after(here3, sent2))
    done, other_b = token_core(1)
    weight_sum3 = weigh(3, after(here3[:, WIDTH:], done), weight_sum2[:, WIDTH:])
    add_up(3, here3)
    with jax.named_scope("bias_grad"):
        mine = jnp.concatenate([column_sums[0] + column_sums[1], column_sums[2] + column_sums[3]]).reshape(4, -1)
        mine = after(mine, weight_sum3)
        other = swap_core(mine)
    done, terms_b = token_x(1, other_b, mine)
    keep_a, zother_a = token_z(terms_a, done)
    with jax.named_scope("bias_grad"):
        other = after(other, keep_a)
        at = (jnp.arange(4)[:, None] == group[None, :])[:, :, None]
        natural = [jnp.sum(jnp.where(at, v[None], 0.0), axis=1) for v in (mine, other)]
        sums = jnp.where(core == 0, jnp.stack(natural, axis=1), jnp.stack(natural[::-1], axis=1)).reshape(-1)
        sums = lax.optimization_barrier(sums)
        opposite = sums + shift_y(sums, 2)
    with jax.named_scope("weight_grad"):
        y1, y3 = after((y1, y3), sums)
        early = lax.optimization_barrier(weight_sum3 + y1.astype(f32) + y3.astype(f32))
    keep_b, zother_b = token_z(terms_b, early)
    with jax.named_scope("bias_grad"):
        opposite = after(opposite, keep_b)
        bias_grad = opposite + shift_y(opposite, 1)
    with jax.named_scope("weight_grad"):
        half = early.shape[0] // 2
        y2 = after(y2, (keep_b, opposite))
        other = swap_core(early[half:] + y2[half:].astype(f32))
        mine = early[:half] + y2[:half].astype(f32)
        weight_grad = jnp.where(
            core == 0, jnp.concatenate([mine, other], axis=1), jnp.concatenate([other, mine], axis=1)
        )
    token_grad = jnp.concatenate([token_last(keep_a, zother_a), token_last(keep_b, zother_b)])
    return (activation, token_grad, weight_grad, bias_grad)


def solution(mesh):
    placed = (P(("depth", "col"), "row"), P("row", "col"), P("col"), P(("depth", "row"), "col"))
    return jax.shard_map(
        body,
        mesh=mesh,
        in_specs=placed,
        out_specs=(
            P(("depth", "row"), "col"),
            P(("depth", "col"), "row"),
            P("row", ("col", "depth")),
            P("col"),
        ),
        check_vma=False,
    )
```

```python
import math

import jax
import jax.numpy as jnp
from jax import lax
from jax.experimental import pallas as pl
from jax.experimental.pallas import tpu as pltpu
from jax.sharding import PartitionSpec as P

gelu_coef = math.sqrt(2.0 / math.pi)
f32 = jnp.float32
bf16 = jnp.bfloat16

ORDER = (1, 3, 2, 0)
WIDTH = 384
PARTS = ((0, 64), (64, 128))
ROUNDS = ((0, 0, 2), (1, 0, 2), (0, 2, 4), (1, 2, 4))
SUM_SIDE = (1, -1)
PIECES = ((0, 0, 2, 1), (1, 0, 2, -1), (2, 2, 4, 1), (3, 2, 4, -1))
CORES = [[0, 2, 4, 6], [1, 3, 5, 7]]


def gelu_parts(preact):
    inner_arg = gelu_coef * (preact + 0.044715 * preact * preact * preact)
    tanh_val = jnp.tanh(inner_arg)
    activation = 0.5 * preact * (1.0 + tanh_val)
    slopes = 0.5 * (1.0 + tanh_val) + 0.5 * preact * (1.0 - tanh_val * tanh_val) * gelu_coef * (
        1.0 + 3.0 * 0.044715 * preact * preact
    )
    return (activation, slopes)


def shift_z(v, by):
    return lax.ppermute(v, "row", [(i, (i + 2 * by) % 8) for i in range(8)])


def swap_core(v):
    return lax.ppermute(v, "row", [(i, i ^ 1) for i in range(8)])


def shift_x(v, by):
    return lax.ppermute(v, "col", [(i, (i + 2 * by) % 8) for i in range(8)])


def swap_z(v):
    return lax.ppermute(v, "col", [(i, i ^ 1) for i in range(8)])


def shift_y(v, by):
    return lax.ppermute(v, "depth", [(i, (i + by) % 4) for i in range(4)])


def split_columns(source, places):
    rows, columns = source.shape
    count = places.shape[0] // 2
    width = columns // places.shape[0]

    def kernel(places_ref, first_in, second_in, first_out, second_out):
        first_out[...] = first_in[...]
        second_out[...] = second_in[...]

    out = jax.ShapeDtypeStruct((rows, count * width), source.dtype)
    return pl.pallas_call(
        kernel,
        grid_spec=pltpu.PrefetchScalarGridSpec(
            num_scalar_prefetch=1,
            grid=(count,),
            in_specs=[
                pl.BlockSpec((rows, width), lambda i, at: (0, at[i])),
                pl.BlockSpec((rows, width), lambda i, at: (0, at[i + count])),
            ],
            out_specs=[pl.BlockSpec((rows, width), lambda i, at: (0, i))] * 2,
        ),
        out_shape=[out, out],
        cost_estimate=pl.CostEstimate(flops=0, bytes_accessed=2 * source.size * source.dtype.itemsize, transcendentals=0),
    )(places, source, source)


def split_small(source, places):
    rows, columns = source.shape
    count = places.shape[0] // 2
    width = columns // places.shape[0]
    tile = min(rows, 128)

    def kernel(at, source_ref, *refs):
        for half, out in enumerate(refs[-2:]):
            for i in range(count):
                start = pl.multiple_of(at[half * count + i] * width, 128)
                out[:, i * width : (i + 1) * width] = source_ref[:, pl.ds(start, width)]

    out = jax.ShapeDtypeStruct((rows, count * width), source.dtype)
    return pl.pallas_call(
        kernel,
        grid_spec=pltpu.PrefetchScalarGridSpec(
            num_scalar_prefetch=1,
            grid=(rows // tile,),
            in_specs=[pl.BlockSpec((tile, columns), lambda i, at: (i, 0))],
            out_specs=[pl.BlockSpec((tile, count * width), lambda i, at: (i, 0))] * 2,
        ),
        out_shape=[out, out],
    )(places, source)


def join_columns(first, second, places):
    rows, columns = first.shape
    count = places.shape[0] // 2
    width = columns // count
    tile = min(rows, 128)

    def kernel(at, first_ref, second_ref, *refs):
        for half, source in enumerate((first_ref, second_ref)):
            for i in range(count):
                start = pl.multiple_of(at[half * count + i] * width, 128)
                refs[-1][:, pl.ds(start, width)] = source[:, i * width : (i + 1) * width]

    return pl.pallas_call(
        kernel,
        grid_spec=pltpu.PrefetchScalarGridSpec(
            num_scalar_prefetch=1,
            grid=(rows // tile,),
            in_specs=[pl.BlockSpec((tile, columns), lambda i, at: (i, 0))] * 2,
            out_specs=pl.BlockSpec((tile, 2 * columns), lambda i, at: (i, 0)),
        ),
        out_shape=jax.ShapeDtypeStruct((rows, 2 * columns), first.dtype),
    )(places, first, second)


def turned(blocks, by):
    n = blocks.shape[0]
    return lax.dynamic_slice_in_dim(jnp.concatenate([blocks, blocks[: n - 1]]), by % n, n, 0)


def after(values, done):
    if done is None:
        return values
    return lax.optimization_barrier((values, done))[0]


def body(tokens, up_weight, hidden_bias, act_grad):
    at_row, at_col, y = lax.axis_index("row"), lax.axis_index("col"), lax.axis_index("depth")
    z, core, x, low = at_row // 2, at_row % 2, at_col // 2, at_col % 2
    group = (y + jnp.array(ORDER, dtype=jnp.int32)) % 4
    places = jnp.concatenate([2 * group + core, 2 * group + 1 - core]).astype(jnp.int32)

    def in_order(mine, other, at):
        return jnp.where(at == 0, jnp.concatenate([mine, other]), jnp.concatenate([other, mine]))

    def gather_pair(part):
        with jax.named_scope("tokens"):
            own = tokens[slice(*PARTS[part])]
            return in_order(own, swap_z(own), low)

    def gather_x(pair):
        with jax.named_scope("tokens"):
            return [pair, shift_x(pair, -1), shift_x(pair, 2), shift_x(pair, 1)]

    def gather_core(around):
        with jax.named_scope("tokens"):
            mine = turned(jnp.stack(around), z - x)
            both = jnp.concatenate([mine, swap_core(mine)], axis=-1)
            return both.reshape(-1, both.shape[-1])

    pair = gather_pair(0)
    with jax.named_scope("weights"):
        kept, sent = split_columns(up_weight, places)
        received = swap_core(sent)
    around = gather_x(after(pair, kept))
    with jax.named_scope("split"):
        kept_grad, sent_grad = split_small(act_grad, places)
        other_grad = swap_core(sent_grad)
        biases, _ = split_small(hidden_bias.astype(f32)[None, :], places)
    with jax.named_scope("weights"):
        weights = {
            cut: jnp.concatenate([part[:, cut[0] * WIDTH : cut[1] * WIDTH] for part in (kept, received)])
            for cut in ((0, 2), (2, 4))
        }
    around = after(around, (kept_grad, biases, weights[0, 2]))
    gathered = [gather_core(around), None]
    activations, column_sums, grads = {}, {}, {}
    token_sums = [None, None]

    def up(k, done):
        part, low_group, high_group = ROUNDS[k]
        with jax.named_scope("up"):
            here = gathered[part] if done is None else after(gathered[part], done)
            return jnp.dot(here, weights[low_group, high_group], preferred_element_type=f32).astype(bf16)

    def scatter(partial):
        with jax.named_scope("sum"):
            natural = turned(partial.reshape(4, -1, partial.shape[-1]), -z).reshape(partial.shape)
            return natural, lax.psum_scatter(natural, "row", scatter_dimension=0, axis_index_groups=CORES, tiled=True)

    def block(partial, j):
        return partial.reshape(4, -1, partial.shape[-1])[j % 4]

    def sum_first(k, partial):
        with jax.named_scope("sum"):
            far, near = lax.optimization_barrier((block(partial, 2), block(partial, -SUM_SIDE[k])))
            return far, shift_z(far, SUM_SIDE[k]), shift_z(near, -SUM_SIDE[k])

    def sum_second(k, partial, passed, near, done):
        with jax.named_scope("sum"):
            passed = after(passed, (near, done))
            total = (block(partial, SUM_SIDE[k]).astype(f32) + passed.astype(f32)).astype(bf16)
            return total, shift_z(total, SUM_SIDE[k])

    def middle(i, terms, done):
        k, low_group, high_group, _ = PIECES[i]
        part, first_group, _ = ROUNDS[k]
        cut = slice(low_group * WIDTH, high_group * WIDTH)
        mine = slice((low_group - first_group) * WIDTH, (high_group - first_group) * WIDTH)
        with jax.named_scope("gelu"):
            terms = [after(terms[0], done)] + terms[1:]
            preact = sum(t[:, mine].astype(f32) for t in terms) + biases[:, cut]
            activation, slopes = gelu_parts(preact)
            grad = (act_grads[part][:, cut].astype(f32) * slopes).astype(bf16)
            grads[i], activations[i] = grad, activation.astype(bf16)
            return grad

    def gather_first(i, done=None):
        side = PIECES[i][3]
        with jax.named_scope("gather"):
            grad = grads[i] if done is None else after(grads[i], done)
            return shift_z(grad, -side), shift_z(grad, side)

    def gather_second(i, near, passed, done):
        side = PIECES[i][3]
        with jax.named_scope("gather"):
            passed, near = after((passed, near), done)
            if i < len(PIECES) - 1:
                passed = after(passed, near)
                far = shift_z(passed, side)
            else:
                half = passed.shape[1] // 2
                far = shift_z(passed[:, :half], side), shift_z(near[:, half:], -side)
                far = jnp.concatenate(far, axis=1)
            blocks = [grads[i], None, far, None]
            blocks[side % 4], blocks[-side % 4] = near, passed
            return passed, blocks

    def whole(blocks, done):
        with jax.named_scope("gather"):
            return lax.optimization_barrier((jnp.concatenate(blocks), done))[0]

    def down(i, here):
        k, low_group, high_group, _ = PIECES[i]
        part = ROUNDS[k][0]
        with jax.named_scope("down"):
            term = lax.dot_general(
                here, weights[low_group, high_group], (((1,), (1,)), ((), ())), preferred_element_type=f32
            )
            token_sums[part] = term if token_sums[part] is None else token_sums[part] + term
            return token_sums[part]

    def weigh(i, here, before=None):
        with jax.named_scope("weight_grad"):
            tokens_here = gathered[ROUNDS[PIECES[i][0]][0]]
            term = lax.dot_general(tokens_here, here, (((0,), (0,)), ((), ())), preferred_element_type=f32)
            return term if before is None else before + term

    def add_up(i, here):
        with jax.named_scope("bias_grad"):
            sums = jnp.sum(here.astype(f32).reshape(4, -1, here.shape[-1]), axis=1)
            column_sums[i] = (sums[0] + sums[2]) + (sums[1] + sums[3])
            return column_sums[i]

    def token_core(part):
        with jax.named_scope("token_grad"):
            half = token_sums[part].shape[1] // 2
            operand = token_sums[part][:, half:].astype(bf16)
            return operand, swap_core(operand)

    def token_x(part, other, done):
        with jax.named_scope("token_grad"):
            half = token_sums[part].shape[1] // 2
            other = after(other, done)
            total = (token_sums[part][:, :half] + other.astype(f32)).astype(bf16)
            total = turned(total.reshape(4, -1, half), x - z)
            return total, [total[0]] + [shift_x(total[i], i) for i in (1, 2, 3)]

    def token_z(terms, done):
        with jax.named_scope("token_grad"):
            terms = after(terms, done)
            total = sum(t.astype(f32) for t in terms)
            rows = total.shape[0] // 2
            keep = jnp.where(low == 0, total[:rows], total[rows:])
            give = jnp.where(low == 0, total[rows:], total[:rows])
            return keep, swap_z(give.astype(bf16))

    def token_last(keep, other):
        with jax.named_scope("token_grad"):
            return (keep + other.astype(f32)).astype(bf16)

    partial0 = up(0, None)
    far0, passed0, near0 = sum_first(0, partial0)
    partial2 = up(2, far0)
    natural2, preact2 = scatter(partial2)
    around = gather_x(after(gather_pair(1), natural2))
    done, far0 = sum_second(0, partial0, passed0, near0, natural2)
    gathered[1] = gather_core(after(around, done))
    partial1 = up(1, None)
    far1, passed1, near1 = sum_first(1, partial1)
    partial3 = up(3, far1)
    natural3, preact3 = scatter(partial3)
    with jax.named_scope("split"):
        other_grad = after(other_grad, done)
        upper, lower = jnp.where(core == 0, kept_grad, other_grad), jnp.where(core == 0, other_grad, kept_grad)
        act_grads = [jnp.concatenate([upper[slice(*p)], lower[slice(*p)]]) for p in PARTS]
    done = middle(0, [far0, near0, block(partial0, 0)], natural3)
    first0 = gather_first(0)
    done, far1 = sum_second(1, partial1, passed1, near1, done)
    done, blocks0 = gather_second(0, *first0, done)
    done = middle(1, [far1, near1, block(partial1, 0)], done)
    first1 = gather_first(1)
    done = middle(2, [preact2], done)
    here0 = whole(blocks0, done)
    weight_sum0 = weigh(0, after(here0, down(0, here0)))
    add_up(0, here0)
    done, blocks1 = gather_second(1, *first1, weight_sum0)
    first2 = gather_first(2, done)
    here1 = whole(blocks1, done)
    weight_sum1 = weigh(1, here1, weight_sum0)
    with jax.named_scope("weight_grad"):
        sent1, sent3 = weight_sum1[:, :WIDTH].astype(bf16), weight_sum1[:, WIDTH:].astype(bf16)
        sent1, sent3 = lax.optimization_barrier((sent1, sent3))
        y1, y3 = shift_y(sent1, 1), shift_y(sent3, 3)
    done = middle(3, [preact3], (sent1, sent3))
    done, blocks2 = gather_second(2, *first2, done)
    first3 = gather_first(3, done)
    done = down(1, after(here1, done))
    add_up(1, here1)
    here2 = whole(blocks2, done)
    down(2, here2)
    done, other_a = token_core(0)
    weight_sum2 = weigh(2, after(here2, done))
    add_up(2, here2)
    with jax.named_scope("activation"):
        pieces = [jnp.concatenate([activations[i], activations[i + 2]], axis=1) for i in (0, 1)]
        rows = pieces[0].shape[0] // 2
        upper = jnp.concatenate([p[:rows] for p in pieces])
        lower = jnp.concatenate([p[rows:] for p in pieces])
        keep, give = jnp.where(core == 0, upper, lower), jnp.where(core == 0, lower, upper)
        keep, give = after((keep, give), weight_sum2)
        other_activation = swap_core(give)
    done, blocks3 = gather_second(3, *first3, (keep, give))
    done, terms_a = token_x(0, other_a, done)
    here3 = whole(blocks3, done)
    with jax.named_scope("weight_grad"):
        sent2 = lax.optimization_barrier(weigh(3, here3[:, :WIDTH], weight_sum2[:, :WIDTH]).astype(bf16))
        y2 = shift_y(sent2, 2)
    down(3, after(here3, sent2))
    done, other_b = token_core(1)
    weight_sum3 = weigh(3, after(here3[:, WIDTH:], done), weight_sum2[:, WIDTH:])
    add_up(3, here3)
    with jax.named_scope("bias_grad"):
        mine = jnp.concatenate([column_sums[0] + column_sums[1], column_sums[2] + column_sums[3]]).reshape(4, -1)
        mine = after(mine, weight_sum3)
        other = swap_core(mine)
    done, terms_b = token_x(1, other_b, mine)
    keep_a, zother_a = token_z(terms_a, done)
    with jax.named_scope("bias_grad"):
        other = after(other, keep_a)
        at = (jnp.arange(4)[:, None] == group[None, :])[:, :, None]
        natural = [jnp.sum(jnp.where(at, v[None], 0.0), axis=1) for v in (mine, other)]
        sums = jnp.where(core == 0, jnp.stack(natural, axis=1), jnp.stack(natural[::-1], axis=1)).reshape(-1)
        sums = lax.optimization_barrier(sums)
        opposite = sums + shift_y(sums, 2)
    with jax.named_scope("activation"):
        activation = join_columns(after(keep, sums), other_activation, places)
    with jax.named_scope("weight_grad"):
        y1, y3 = after((y1, y3), activation)
        early = lax.optimization_barrier(weight_sum3 + y1.astype(f32) + y3.astype(f32))
    keep_b, zother_b = token_z(terms_b, early)
    with jax.named_scope("bias_grad"):
        opposite = after(opposite, keep_b)
        bias_grad = opposite + shift_y(opposite, 1)
    with jax.named_scope("weight_grad"):
        half = early.shape[0] // 2
        y2 = after(y2, (keep_b, opposite))
        other = swap_core(early[half:] + y2[half:].astype(f32))
        mine = early[:half] + y2[:half].astype(f32)
        weight_grad = jnp.where(
            core == 0, jnp.concatenate([mine, other], axis=1), jnp.concatenate([other, mine], axis=1)
        )
    zother_a = after(zother_a, keep_b)
    token_grad = jnp.concatenate([token_last(keep_a, zother_a), token_last(keep_b, zother_b)])
    return (activation, token_grad, weight_grad, bias_grad)


def solution(mesh):
    placed = (P(("depth", "col"), "row"), P("row", "col"), P("col"), P(("depth", "row"), "col"))
    return jax.shard_map(
        body,
        mesh=mesh,
        in_specs=placed,
        out_specs=(
            P(("depth", "row"), "col"),
            P(("depth", "col"), "row"),
            P("row", ("col", "depth")),
            P("col"),
        ),
        check_vma=False,
    )
```

```python
import math

import jax
import jax.numpy as jnp
from jax import lax
from jax.experimental import pallas as pl
from jax.experimental.pallas import tpu as pltpu
from jax.sharding import PartitionSpec as P

gelu_coef = math.sqrt(2.0 / math.pi)
f32 = jnp.float32
bf16 = jnp.bfloat16

ORDER = (1, 3, 2, 0)
WIDTH = 384
PARTS = ((0, 64), (64, 128))
ROUNDS = ((0, 0, 2), (1, 0, 2), (0, 2, 4), (1, 2, 4))
SUM_SIDE = (1, -1)
PIECES = ((0, 0, 2, 1), (1, 0, 2, -1), (2, 2, 4, 1), (3, 2, 4, -1))
CORES = [[0, 2, 4, 6], [1, 3, 5, 7]]


def gelu_parts(preact):
    inner_arg = gelu_coef * (preact + 0.044715 * preact * preact * preact)
    tanh_val = jnp.tanh(inner_arg)
    activation = 0.5 * preact * (1.0 + tanh_val)
    slopes = 0.5 * (1.0 + tanh_val) + 0.5 * preact * (1.0 - tanh_val * tanh_val) * gelu_coef * (
        1.0 + 3.0 * 0.044715 * preact * preact
    )
    return (activation, slopes)


def shift_z(v, by):
    return lax.ppermute(v, "row", [(i, (i + 2 * by) % 8) for i in range(8)])


def swap_core(v):
    return lax.ppermute(v, "row", [(i, i ^ 1) for i in range(8)])


def shift_x(v, by):
    return lax.ppermute(v, "col", [(i, (i + 2 * by) % 8) for i in range(8)])


def swap_z(v):
    return lax.ppermute(v, "col", [(i, i ^ 1) for i in range(8)])


def shift_y(v, by):
    return lax.ppermute(v, "depth", [(i, (i + by) % 4) for i in range(4)])


def split_columns(source, places):
    rows, columns = source.shape
    count = places.shape[0] // 2
    width = columns // places.shape[0]

    def kernel(places_ref, first_in, second_in, first_out, second_out):
        first_out[...] = first_in[...]
        second_out[...] = second_in[...]

    out = jax.ShapeDtypeStruct((rows, count * width), source.dtype)
    return pl.pallas_call(
        kernel,
        grid_spec=pltpu.PrefetchScalarGridSpec(
            num_scalar_prefetch=1,
            grid=(count,),
            in_specs=[
                pl.BlockSpec((rows, width), lambda i, at: (0, at[i])),
                pl.BlockSpec((rows, width), lambda i, at: (0, at[i + count])),
            ],
            out_specs=[pl.BlockSpec((rows, width), lambda i, at: (0, i))] * 2,
        ),
        out_shape=[out, out],
        cost_estimate=pl.CostEstimate(flops=0, bytes_accessed=2 * source.size * source.dtype.itemsize, transcendentals=0),
    )(places, source, source)


def split_small(source, places):
    rows, columns = source.shape
    count = places.shape[0] // 2
    width = columns // places.shape[0]
    tile = min(rows, 128)

    def kernel(at, source_ref, *refs):
        for half, out in enumerate(refs[-2:]):
            for i in range(count):
                start = pl.multiple_of(at[half * count + i] * width, 128)
                out[:, i * width : (i + 1) * width] = source_ref[:, pl.ds(start, width)]

    out = jax.ShapeDtypeStruct((rows, count * width), source.dtype)
    return pl.pallas_call(
        kernel,
        grid_spec=pltpu.PrefetchScalarGridSpec(
            num_scalar_prefetch=1,
            grid=(rows // tile,),
            in_specs=[pl.BlockSpec((tile, columns), lambda i, at: (i, 0))],
            out_specs=[pl.BlockSpec((tile, count * width), lambda i, at: (i, 0))] * 2,
        ),
        out_shape=[out, out],
    )(places, source)


def join_columns(first, second, places):
    rows, columns = first.shape
    count = places.shape[0] // 2
    width = columns // count
    tile = min(rows, 128)

    def kernel(at, first_ref, second_ref, *refs):
        for half, source in enumerate((first_ref, second_ref)):
            for i in range(count):
                start = pl.multiple_of(at[half * count + i] * width, 128)
                refs[-1][:, pl.ds(start, width)] = source[:, i * width : (i + 1) * width]

    return pl.pallas_call(
        kernel,
        grid_spec=pltpu.PrefetchScalarGridSpec(
            num_scalar_prefetch=1,
            grid=(rows // tile,),
            in_specs=[pl.BlockSpec((tile, columns), lambda i, at: (i, 0))] * 2,
            out_specs=pl.BlockSpec((tile, 2 * columns), lambda i, at: (i, 0)),
        ),
        out_shape=jax.ShapeDtypeStruct((rows, 2 * columns), first.dtype),
    )(places, first, second)


def turned(blocks, by):
    n = blocks.shape[0]
    return lax.dynamic_slice_in_dim(jnp.concatenate([blocks, blocks[: n - 1]]), by % n, n, 0)


def after(values, done):
    if done is None:
        return values
    return lax.optimization_barrier((values, done))[0]


def body(tokens, up_weight, hidden_bias, act_grad):
    at_row, at_col, y = lax.axis_index("row"), lax.axis_index("col"), lax.axis_index("depth")
    z, core, x, low = at_row // 2, at_row % 2, at_col // 2, at_col % 2
    group = (y + jnp.array(ORDER, dtype=jnp.int32)) % 4
    places = jnp.concatenate([2 * group + core, 2 * group + 1 - core]).astype(jnp.int32)

    def in_order(mine, other, at):
        return jnp.where(at == 0, jnp.concatenate([mine, other]), jnp.concatenate([other, mine]))

    def gather_pair(part):
        with jax.named_scope("tokens"):
            own = tokens[slice(*PARTS[part])]
            return in_order(own, swap_z(own), low)

    def gather_x(pair):
        with jax.named_scope("tokens"):
            return [pair, shift_x(pair, -1), shift_x(pair, 2), shift_x(pair, 1)]

    def gather_core(around):
        with jax.named_scope("tokens"):
            mine = turned(jnp.stack(around), z - x)
            both = jnp.concatenate([mine, swap_core(mine)], axis=-1)
            return both.reshape(-1, both.shape[-1])

    pair = gather_pair(0)
    with jax.named_scope("weights"):
        kept, sent = split_columns(up_weight, places)
        received = swap_core(sent)
    around = gather_x(after(pair, kept))
    with jax.named_scope("split"):
        kept_grad, sent_grad = split_small(act_grad, places)
        other_grad = swap_core(sent_grad)
        biases, _ = split_small(hidden_bias.astype(f32)[None, :], places)
    with jax.named_scope("weights"):
        weights = {
            cut: jnp.concatenate([part[:, cut[0] * WIDTH : cut[1] * WIDTH] for part in (kept, received)])
            for cut in ((0, 2), (2, 4))
        }
    around = after(around, (kept_grad, biases, weights[0, 2]))
    gathered = [gather_core(around), None]
    activations, column_sums, grads = {}, {}, {}
    token_sums = [None, None]

    def up(k, done):
        part, low_group, high_group = ROUNDS[k]
        with jax.named_scope("up"):
            here = gathered[part] if done is None else after(gathered[part], done)
            return jnp.dot(here, weights[low_group, high_group], preferred_element_type=f32).astype(bf16)

    def scatter(partial):
        with jax.named_scope("sum"):
            natural = turned(partial.reshape(4, -1, partial.shape[-1]), -z).reshape(partial.shape)
            return natural, lax.psum_scatter(natural, "row", scatter_dimension=0, axis_index_groups=CORES, tiled=True)

    def block(partial, j):
        return partial.reshape(4, -1, partial.shape[-1])[j % 4]

    def sum_first(k, partial):
        with jax.named_scope("sum"):
            far, near = lax.optimization_barrier((block(partial, 2), block(partial, -SUM_SIDE[k])))
            return far, shift_z(far, SUM_SIDE[k]), shift_z(near, -SUM_SIDE[k])

    def sum_second(k, partial, passed, near, done):
        with jax.named_scope("sum"):
            passed = after(passed, (near, done))
            total = (block(partial, SUM_SIDE[k]).astype(f32) + passed.astype(f32)).astype(bf16)
            return total, shift_z(total, SUM_SIDE[k])

    def middle(i, terms, done):
        k, low_group, high_group, _ = PIECES[i]
        part, first_group, _ = ROUNDS[k]
        cut = slice(low_group * WIDTH, high_group * WIDTH)
        mine = slice((low_group - first_group) * WIDTH, (high_group - first_group) * WIDTH)
        with jax.named_scope("gelu"):
            terms = [after(terms[0], done)] + terms[1:]
            preact = sum(t[:, mine].astype(f32) for t in terms) + biases[:, cut]
            activation, slopes = gelu_parts(preact)
            grad = (act_grads[part][:, cut].astype(f32) * slopes).astype(bf16)
            grads[i], activations[i] = grad, activation.astype(bf16)
            return grad

    def gather_first(i, done=None):
        side = PIECES[i][3]
        with jax.named_scope("gather"):
            grad = grads[i] if done is None else after(grads[i], done)
            return shift_z(grad, -side), shift_z(grad, side)

    def gather_second(i, near, passed, done):
        side = PIECES[i][3]
        with jax.named_scope("gather"):
            passed, near = after((passed, near), done)
            if i < len(PIECES) - 1:
                passed = after(passed, near)
                far = shift_z(passed, side)
            else:
                half = passed.shape[1] // 2
                far = shift_z(passed[:, :half], side), shift_z(near[:, half:], -side)
                far = jnp.concatenate(far, axis=1)
            blocks = [grads[i], None, far, None]
            blocks[side % 4], blocks[-side % 4] = near, passed
            return passed, blocks

    def whole(blocks, done):
        with jax.named_scope("gather"):
            return lax.optimization_barrier((jnp.concatenate(blocks), done))[0]

    def down(i, here):
        k, low_group, high_group, _ = PIECES[i]
        part = ROUNDS[k][0]
        with jax.named_scope("down"):
            term = lax.dot_general(
                here, weights[low_group, high_group], (((1,), (1,)), ((), ())), preferred_element_type=f32
            )
            token_sums[part] = term if token_sums[part] is None else token_sums[part] + term
            return token_sums[part]

    def weigh(i, here, before=None):
        with jax.named_scope("weight_grad"):
            tokens_here = gathered[ROUNDS[PIECES[i][0]][0]]
            term = lax.dot_general(tokens_here, here, (((0,), (0,)), ((), ())), preferred_element_type=f32)
            return term if before is None else before + term

    def add_up(i, here):
        with jax.named_scope("bias_grad"):
            sums = jnp.sum(here.astype(f32).reshape(4, -1, here.shape[-1]), axis=1)
            column_sums[i] = (sums[0] + sums[2]) + (sums[1] + sums[3])
            return column_sums[i]

    def token_core(part):
        with jax.named_scope("token_grad"):
            half = token_sums[part].shape[1] // 2
            operand = token_sums[part][:, half:].astype(bf16)
            return operand, swap_core(operand)

    def token_x(part, other, done):
        with jax.named_scope("token_grad"):
            half = token_sums[part].shape[1] // 2
            other = after(other, done)
            total = (token_sums[part][:, :half] + other.astype(f32)).astype(bf16)
            total = turned(total.reshape(4, -1, half), x - z)
            return total, [total[0]] + [shift_x(total[i], i) for i in (1, 2, 3)]

    def token_z(terms, done):
        with jax.named_scope("token_grad"):
            terms = after(terms, done)
            total = sum(t.astype(f32) for t in terms)
            rows = total.shape[0] // 2
            keep = jnp.where(low == 0, total[:rows], total[rows:])
            give = jnp.where(low == 0, total[rows:], total[:rows])
            return keep, swap_z(give.astype(bf16))

    def token_last(keep, other):
        with jax.named_scope("token_grad"):
            return (keep + other.astype(f32)).astype(bf16)

    partial0 = up(0, None)
    far0, passed0, near0 = sum_first(0, partial0)
    partial2 = up(2, far0)
    natural2, preact2 = scatter(partial2)
    around = gather_x(after(gather_pair(1), natural2))
    done, far0 = sum_second(0, partial0, passed0, near0, natural2)
    gathered[1] = gather_core(after(around, done))
    partial1 = up(1, None)
    far1, passed1, near1 = sum_first(1, partial1)
    partial3 = up(3, far1)
    natural3, preact3 = scatter(partial3)
    with jax.named_scope("split"):
        other_grad = after(other_grad, done)
        upper, lower = jnp.where(core == 0, kept_grad, other_grad), jnp.where(core == 0, other_grad, kept_grad)
        act_grads = [jnp.concatenate([upper[slice(*p)], lower[slice(*p)]]) for p in PARTS]
    done = middle(0, [far0, near0, block(partial0, 0)], natural3)
    first0 = gather_first(0)
    done, far1 = sum_second(1, partial1, passed1, near1, done)
    done, blocks0 = gather_second(0, *first0, done)
    done = middle(1, [far1, near1, block(partial1, 0)], done)
    first1 = gather_first(1)
    done = middle(2, [preact2], done)
    here0 = whole(blocks0, done)
    weight_sum0 = weigh(0, after(here0, down(0, here0)))
    add_up(0, here0)
    done, blocks1 = gather_second(1, *first1, weight_sum0)
    first2 = gather_first(2, done)
    here1 = whole(blocks1, done)
    weight_sum1 = weigh(1, here1, weight_sum0)
    with jax.named_scope("weight_grad"):
        sent1, sent3 = weight_sum1[:, :WIDTH].astype(bf16), weight_sum1[:, WIDTH:].astype(bf16)
        sent1, sent3 = lax.optimization_barrier((sent1, sent3))
        y1, y3 = shift_y(sent1, 1), shift_y(sent3, 3)
    done = middle(3, [preact3], (sent1, sent3))
    done, blocks2 = gather_second(2, *first2, done)
    first3 = gather_first(3, done)
    done = down(1, after(here1, done))
    add_up(1, here1)
    here2 = whole(blocks2, done)
    down(2, here2)
    done, other_a = token_core(0)
    weight_sum2 = weigh(2, after(here2, done))
    add_up(2, here2)
    with jax.named_scope("activation"):
        pieces = [jnp.concatenate([activations[i], activations[i + 2]], axis=1) for i in (0, 1)]
        rows = pieces[0].shape[0] // 2
        upper = jnp.concatenate([p[:rows] for p in pieces])
        lower = jnp.concatenate([p[rows:] for p in pieces])
        keep, give = jnp.where(core == 0, upper, lower), jnp.where(core == 0, lower, upper)
        keep, give = after((keep, give), weight_sum2)
        other_activation = swap_core(give)
    done, blocks3 = gather_second(3, *first3, (keep, give))
    done, terms_a = token_x(0, other_a, done)
    here3 = whole(blocks3, (done, y1, y3))
    with jax.named_scope("weight_grad"):
        sent2 = lax.optimization_barrier(weigh(3, here3[:, :WIDTH], weight_sum2[:, :WIDTH]).astype(bf16))
        y2 = shift_y(sent2, 2)
    down(3, after(here3, sent2))
    done, other_b = token_core(1)
    weight_sum3 = weigh(3, after(here3[:, WIDTH:], done), weight_sum2[:, WIDTH:])
    add_up(3, here3)
    with jax.named_scope("bias_grad"):
        mine = jnp.concatenate([column_sums[0] + column_sums[1], column_sums[2] + column_sums[3]]).reshape(4, -1)
        mine = after(mine, weight_sum3)
        other = swap_core(mine)
    done, terms_b = token_x(1, other_b, mine)
    keep_a, zother_a = token_z(terms_a, done)
    with jax.named_scope("bias_grad"):
        other = after(other, keep_a)
        at = (jnp.arange(4)[:, None] == group[None, :])[:, :, None]
        natural = [jnp.sum(jnp.where(at, v[None], 0.0), axis=1) for v in (mine, other)]
        sums = jnp.where(core == 0, jnp.stack(natural, axis=1), jnp.stack(natural[::-1], axis=1)).reshape(-1)
        sums = lax.optimization_barrier(sums)
        opposite = sums + shift_y(sums, 2)
    with jax.named_scope("activation"):
        activation = join_columns(after(keep, sums), other_activation, places)
    with jax.named_scope("weight_grad"):
        y1, y3 = after((y1, y3), activation)
        early = lax.optimization_barrier(weight_sum3 + y1.astype(f32) + y3.astype(f32))
    keep_b, zother_b = token_z(terms_b, early)
    with jax.named_scope("bias_grad"):
        opposite = after(opposite, keep_b)
        bias_grad = opposite + shift_y(opposite, 1)
    with jax.named_scope("weight_grad"):
        half = early.shape[0] // 2
        y2 = after(y2, (keep_b, opposite))
        other = swap_core(early[half:] + y2[half:].astype(f32))
        mine = early[:half] + y2[:half].astype(f32)
        weight_grad = jnp.where(
            core == 0, jnp.concatenate([mine, other], axis=1), jnp.concatenate([other, mine], axis=1)
        )
    zother_a = after(zother_a, keep_b)
    token_grad = jnp.concatenate([token_last(keep_a, zother_a), token_last(keep_b, zother_b)])
    return (activation, token_grad, weight_grad, bias_grad)


def solution(mesh):
    placed = (P(("depth", "col"), "row"), P("row", "col"), P("col"), P(("depth", "row"), "col"))
    return jax.shard_map(
        body,
        mesh=mesh,
        in_specs=placed,
        out_specs=(
            P(("depth", "row"), "col"),
            P(("depth", "col"), "row"),
            P("row", ("col", "depth")),
            P("col"),
        ),
        check_vma=False,
    )
```
